32 devices in a mesh: rep: 2 (over y), dp: 4 (over x, core), tensor: 4 (over z).
Axes of the slice: x: 2, y: 2, z: 4, core: 2. Of those that a mesh axis runs over, the one named last changes fastest.
Arguments:
- attention: bfloat16 [3, 2048, 8192], P(None, ('rep', 'dp'), 'tensor'), parts along dimension 1, may hold values from -6 to 6
- residual: bfloat16 [3, 2048, 8192], P(None, ('rep', 'dp'), 'tensor'), parts along dimension 1, may hold values from -6 to 6
- output_weight: bfloat16 [8192, 8192], P('tensor'), may hold values from -0.09375 to 0.09375
- adapter_down_maps: bfloat16 [1024, 16, 8192], P('dp', None, 'tensor'), may hold values from -0.0625 to 0.0625
- adapter_up_maps: bfloat16 [1024, 16, 8192], P('dp', None, 'tensor'), may hold values from -1.5 to 1.5
- lacking_adapter_lists: int32 [3, 8, 4, 16], P(None, ('rep', 'dp')), parts along dimension 1, may hold values from 0 to 255
- request_slot_index: int32 [3, 2048], P(None, ('rep', 'dp')), parts along dimension 1, may hold values from 0 to 63
Outputs:
- mixed: bfloat16 [3, 2048, 8192], P(None, ('rep', 'dp'), 'tensor'), parts along dimension 1
The draws below stay inside these ranges and needn't reach their ends.
There are 2 independent parts, one for each index of `rep`. The reference program is written for one: setup_inputs(seed, part) draws one part's arguments, and reference() takes and returns one part's arrays. A program takes and returns all parts, laid end to end along the dimension named above; an argument that names none is the same for every part. Nothing has to cross between parts.
All inputs are finite; a program needn't handle non-finite values.
Results may differ from the reference program's by a relative error of at most 0.011.
Values may be sent and summed in bfloat16 or wider, within the bound.
A program may use at most 256 MiB of HBM per device.

```python
import jax
import jax.numpy as jnp
from jax import lax

MODEL_WIDTH = 8192
ADAPTER_RANK = 16
ROWS = 256
STEPS = 3
ADP_GRP = 256
MISS = 16
TOKENS = 1024
ADAPTER_TOTAL = 1024
SLOTS = 64
N_DP = 4
N_TENSOR = 4


def set_ends(array, rng, smallest, high):
    dims = array.shape
    spot = [jax.random.randint(jax.random.fold_in(rng, axis), (), 0, dims[axis]) for axis in range(len(dims))]
    array = array.at[tuple(spot)].set(smallest)
    longest = dims.index(max(dims))
    spot[longest] = (spot[longest] + 1) % dims[longest]
    return array.at[tuple(spot)].set(high)


def strengthened(array, own_key, source, target, blocks, factor):
    owner, partner = [(jnp.arange(array.shape[axis_at]) // (array.shape[axis_at] // blocks)).reshape([-1 if axis == axis_at else 1 for axis in range(array.ndim)]) for axis_at in (source, target)]
    chosen = jax.random.permutation(own_key, blocks)[partner]
    strong = (owner == chosen) | (owner == (partner + blocks // 2) % blocks)
    return jnp.where(strong, factor * array, array)


def levels(own_key, extent, shards, least, high):
    factor_of = 1.0
    for dim, blocks in shards:
        draws = jax.random.uniform(jax.random.fold_in(jax.random.fold_in(own_key, 6), dim), (blocks,), jnp.float32, least / len(shards), high / len(shards))
        factor_of = factor_of * jnp.repeat(jnp.exp(draws), extent[dim] // blocks).reshape((-1,) + (1,) * (len(extent) - 1 - dim))
    return factor_of


def scatter_about(stream_key, extent, width, limit, shards=(), kind=jnp.bfloat16):
    loudness = levels(stream_key, extent, shards, -0.22, 0.18) if shards else 1.0
    result = jax.random.normal(stream_key, extent, jnp.float32) * width * loudness
    return jnp.minimum(jnp.maximum(result, -limit), limit).astype(kind)


def noise_with(key, extent, deviation, bound, split, heavy, held_as=jnp.bfloat16):
    result = deviation * jax.random.normal(key, extent, jnp.float32)
    if split:
        result = result * levels(key, extent, split, -0.22, 0.18)
    return jnp.clip(strengthened(result, jax.random.fold_in(key, 3), *heavy), -bound, bound).astype(held_as)


def setup_inputs(seed: int = 0, part: int = 0) -> dict:
    seeds = jax.random.split(jax.random.key(seed), 8)
    own_keys = jax.random.split(jax.random.fold_in(seeds[7], part), 8)
    return {
        "attention": scatter_about(own_keys[0], (STEPS, TOKENS, MODEL_WIDTH), 1.0, 6.0, ((1, 4), (2, 4))),
        "residual": scatter_about(own_keys[1], (STEPS, TOKENS, MODEL_WIDTH), 1.0, 6.0, ((1, 4), (2, 4))),
        "output_weight": noise_with(seeds[2], (MODEL_WIDTH, MODEL_WIDTH), MODEL_WIDTH ** -0.5, 0.09375, ((0, 4),), (0, 1, 4, 2.0)),
        "adapter_down_maps": scatter_about(seeds[3], (ADAPTER_TOTAL, ADAPTER_RANK, MODEL_WIDTH), MODEL_WIDTH ** -0.5, 0.0625, ((0, 4), (2, 4))),
        "adapter_up_maps": scatter_about(seeds[4], (ADAPTER_TOTAL, ADAPTER_RANK, MODEL_WIDTH), ADAPTER_RANK ** -0.5, 1.5, ((0, 4), (2, 4))),
        "lacking_adapter_lists": set_ends(jax.random.randint(own_keys[5], (STEPS, N_DP, N_DP, MISS), 0, ADP_GRP), jax.random.fold_in(own_keys[5], 1), 0, ADP_GRP - 1).astype(jnp.int32),
        "request_slot_index": set_ends(jax.random.randint(own_keys[6], (STEPS, TOKENS), 0, SLOTS), jax.random.fold_in(own_keys[6], 1), 0, SLOTS - 1).astype(jnp.int32),
    }


adapter_scale = 2.0


def reference(attention, residual, output_weight, adapter_down_maps, adapter_up_maps, lacking_adapter_lists, request_slot_index):
    width_dev = MODEL_WIDTH // N_TENSOR
    row_group = jnp.arange(TOKENS, dtype=jnp.int32) // ROWS
    outputs = []
    for step_index in range(STEPS):
        slot_ids = request_slot_index[step_index]
        owner_id = slot_ids // MISS
        local_id = lacking_adapter_lists[step_index][row_group, owner_id, slot_ids % MISS]
        adapter_index = (owner_id * ADP_GRP + local_id).astype(jnp.int32)
        inputs = attention[step_index]
        request_down_maps = adapter_down_maps[adapter_index]

        def shard_terms(carry, shard):
            start = (shard * width_dev).astype(jnp.int32)
            input_part = lax.dynamic_slice_in_dim(inputs, start, width_dev, 1)
            weight_part = lax.dynamic_slice_in_dim(output_weight, start, width_dev, 0)
            down_part = lax.dynamic_slice_in_dim(request_down_maps, start, width_dev, 2)
            base_part = jnp.dot(input_part, weight_part, preferred_element_type=jnp.float32)
            base_part = lax.optimization_barrier(base_part.astype(jnp.bfloat16)).astype(jnp.float32)
            shrink_part = jnp.einsum("td,trd->tr", input_part.astype(jnp.float32), down_part.astype(jnp.float32))
            shrink_part = lax.optimization_barrier(shrink_part.astype(jnp.bfloat16)).astype(jnp.float32)
            return (carry[0] + base_part, carry[1] + shrink_part), None

        start_carry = (jnp.zeros((TOKENS, MODEL_WIDTH), jnp.float32), jnp.zeros((TOKENS, ADAPTER_RANK), jnp.float32))
        (projected_output, shrink_sum), _ = lax.scan(shard_terms, start_carry, jnp.arange(N_TENSOR, dtype=jnp.int32))
        rank_reduced = shrink_sum.astype(jnp.bfloat16)
        request_up_maps = adapter_up_maps[adapter_index]
        adapter_output = jnp.einsum("ly,lyb->lb", rank_reduced.astype(jnp.float32), request_up_maps.astype(jnp.float32))
        mixed = residual[step_index].astype(jnp.float32) + projected_output + adapter_scale * adapter_output
        outputs.append(mixed.astype(jnp.bfloat16))
    return jnp.stack(outputs)
```

```python
import functools

import jax
import jax.numpy as jnp
from jax import lax
from jax.experimental import pallas as pl
from jax.experimental.pallas import tpu as pltpu
from jax.sharding import PartitionSpec as P

adapter_scale = 2.0
MESH = pl.DeviceIdType.MESH


def project_kernel(
    n, per_block, tile, a_ref, w_hbm, o_ref, w_buf, part, from_left, from_right,
    w_sem, left_sem, right_sem, to_right_sem, to_left_sem,
):
    me = lax.axis_index("tensor")
    steps = (n - 1) * per_block

    def fetch(t):
        return pltpu.make_async_copy(
            w_hbm.at[:, pl.ds(pl.multiple_of(t * tile, tile), tile)], w_buf.at[t], w_sem.at[t]
        )

    def send_right(t):
        return pltpu.make_async_remote_copy(
            src_ref=from_left.at[t], dst_ref=from_left.at[t],
            send_sem=to_right_sem.at[t], recv_sem=left_sem.at[t],
            device_id={"tensor": me + 1}, device_id_type=MESH,
        )

    def send_left(t):
        return pltpu.make_async_remote_copy(
            src_ref=from_right.at[t], dst_ref=from_right.at[t],
            send_sem=to_left_sem.at[t], recv_sem=right_sem.at[t],
            device_id={"tensor": me - 1}, device_id_type=MESH,
        )

    def blocks(i):
        turn, piece = i // per_block, i % per_block
        return n - 1 - turn, turn, piece

    def fetch_step(i, carry):
        right_block, left_block, piece = blocks(i)

        @pl.when(right_block > me)
        def _():
            fetch(right_block * per_block + piece).start()

        @pl.when(left_block < me)
        def _():
            fetch(left_block * per_block + piece).start()

        return carry

    def fetch_own(i, carry):
        fetch(me * per_block + i).start()
        return carry

    lax.fori_loop(0, steps, fetch_step, 0)
    lax.fori_loop(0, per_block, fetch_own, 0)

    barrier = pltpu.get_barrier_semaphore()

    @pl.when(me > 0)
    def _():
        pl.semaphore_signal(barrier, inc=1, device_id={"tensor": me - 1}, device_id_type=MESH)

    @pl.when(me < n - 1)
    def _():
        pl.semaphore_signal(barrier, inc=1, device_id={"tensor": me + 1}, device_id_type=MESH)

    peers = (me > 0).astype(jnp.int32) + (me < n - 1).astype(jnp.int32)
    pl.semaphore_wait(barrier, peers)

    def product(t):
        fetch(t).wait()
        part[...] = jnp.dot(a_ref[...], w_buf[t], preferred_element_type=jnp.float32)

    def step(i, carry):
        right_block, left_block, piece = blocks(i)

        @pl.when(right_block > me)
        def _():
            t = right_block * per_block + piece
            product(t)

            @pl.when(me > 0)
            def _():
                send_right(t).wait_recv()
                part[...] += from_left[t].astype(jnp.float32)

            from_left[t] = part[...].astype(jnp.bfloat16)
            send_right(t).start()

        @pl.when(left_block < me)
        def _():
            t = left_block * per_block + piece
            product(t)

            @pl.when(me < n - 1)
            def _():
                send_left(t).wait_recv()
                part[...] += from_right[t].astype(jnp.float32)

            from_right[t] = part[...].astype(jnp.bfloat16)
            send_left(t).start()

        return carry

    lax.fori_loop(0, steps, step, 0)

    def own(i, carry):
        t = me * per_block + i
        product(t)

        @pl.when(me > 0)
        def _():
            send_right(t).wait_recv()
            part[...] += from_left[t].astype(jnp.float32)

        @pl.when(me < n - 1)
        def _():
            send_left(t).wait_recv()
            part[...] += from_right[t].astype(jnp.float32)

        o_ref[i] = part[...]
        return carry

    lax.fori_loop(0, per_block, own, 0)

    def drain(i, carry):
        right_block, left_block, piece = blocks(i)

        @pl.when(right_block > me)
        def _():
            send_right(right_block * per_block + piece).wait_send()

        @pl.when(left_block < me)
        def _():
            send_left(left_block * per_block + piece).wait_send()

        return carry

    lax.fori_loop(0, steps, drain, 0)


def project(inputs, weight, n, collective_id):
    rows, depth = inputs.shape
    columns = weight.shape[1]
    width = columns // n
    tile = min(256, width)
    per_block = width // tile
    tiles = n * per_block
    return pl.pallas_call(
        functools.partial(project_kernel, n, per_block, tile),
        out_shape=jax.ShapeDtypeStruct((per_block, rows, tile), jnp.float32),
        in_specs=[
            pl.BlockSpec(memory_space=pltpu.VMEM),
            pl.BlockSpec(memory_space=pl.ANY),
        ],
        out_specs=pl.BlockSpec(memory_space=pltpu.VMEM),
        scratch_shapes=[
            pltpu.VMEM((tiles, depth, tile), jnp.bfloat16),
            pltpu.VMEM((rows, tile), jnp.float32),
            pltpu.VMEM((tiles, rows, tile), jnp.bfloat16),
            pltpu.VMEM((tiles, rows, tile), jnp.bfloat16),
            pltpu.SemaphoreType.DMA((tiles,)),
            pltpu.SemaphoreType.DMA((tiles,)),
            pltpu.SemaphoreType.DMA((tiles,)),
            pltpu.SemaphoreType.DMA((tiles,)),
            pltpu.SemaphoreType.DMA((tiles,)),
        ],
        compiler_params=pltpu.CompilerParams(
            collective_id=collective_id, has_side_effects=True, vmem_limit_bytes=60 * 2**20
        ),
        cost_estimate=pl.CostEstimate(
            flops=2 * rows * depth * columns,
            bytes_accessed=2 * depth * columns + 64 * rows * width,
            transcendentals=0,
        ),
    )(inputs, weight)


def shards(
    groups,
    n,
    attention,
    residual,
    output_weight,
    adapter_down_maps,
    adapter_up_maps,
    lacking_adapter_lists,
    request_slot_index,
):
    step_count, row_count, feature_count = attention.shape
    rank = adapter_down_maps.shape[1]
    width = residual.shape[2]
    owners, per_owner = lacking_adapter_lists.shape[2:]
    me = lax.axis_index("dp")

    everyone = lax.all_gather(attention, "dp", axis=0)
    small = jnp.concatenate(
        [lacking_adapter_lists[:, 0].reshape(step_count, -1), request_slot_index], axis=1
    )
    small = lax.all_gather(small, "dp", axis=0)
    wanted = small[:, :, : owners * per_owner].reshape(groups, step_count, owners, per_owner)
    wanted = lax.dynamic_index_in_dim(wanted, me, axis=2, keepdims=False)
    slots = small[:, :, owners * per_owner :] - me * per_owner
    down_now = jnp.take(adapter_down_maps, wanted, axis=0).reshape(
        groups, step_count, per_owner * rank, feature_count
    )
    up_now = jnp.take(adapter_up_maps, wanted, axis=0).reshape(
        groups, step_count, per_owner * rank, width
    )

    first = project(attention[0], output_weight, n, 1)

    mine = slots[..., None] == jnp.arange(per_owner, dtype=jnp.int32)
    everyone, first = lax.optimization_barrier((everyone, first))
    shrink_all = lax.dot_general(
        everyone, down_now, (((3,), (3,)), ((0, 1), (0, 1))), preferred_element_type=jnp.float32
    ).reshape(groups, step_count, row_count, per_owner, rank)
    picked = jnp.sum(jnp.where(mine[..., None], shrink_all, 0.0), axis=3)
    shrink = lax.psum(picked.astype(jnp.bfloat16), "tensor")
    expanded = jnp.where(mine[..., None], shrink[:, :, :, None, :], jnp.zeros((), jnp.bfloat16))
    expanded = expanded.reshape(groups, step_count, row_count, per_owner * rank)
    lora = lax.dot_general(
        expanded, up_now, (((3,), (2,)), ((0, 1), (0, 1))), preferred_element_type=jnp.float32
    ).astype(jnp.bfloat16)

    lora, rest_in = lax.optimization_barrier(
        (lora, attention[1:].reshape((step_count - 1) * row_count, feature_count))
    )
    rest = project(rest_in, output_weight, n, 2)
    lora_own = lax.psum_scatter(lora, "dp", scatter_dimension=0, tiled=False)

    def placed(pieces, steps):
        per_block, rows, tile = pieces.shape
        return pieces.transpose(1, 0, 2).reshape(steps, row_count, per_block * tile)

    projected = jnp.concatenate([placed(first, 1), placed(rest, step_count - 1)], axis=0)
    mixed = (
        residual.astype(jnp.float32)
        + projected
        + adapter_scale * lora_own.astype(jnp.float32)
    )
    return mixed.astype(jnp.bfloat16)


def solution(mesh):
    placed = (
        P(None, ("rep", "dp"), "tensor"),
        P(None, ("rep", "dp"), "tensor"),
        P("tensor", None),
        P("dp", None, "tensor"),
        P("dp", None, "tensor"),
        P(None, ("rep", "dp"), None, None),
        P(None, ("rep", "dp")),
    )
    return jax.shard_map(
        functools.partial(shards, mesh.shape["dp"], mesh.shape["tensor"]),
        mesh=mesh,
        in_specs=placed,
        out_specs=P(None, ("rep", "dp"), "tensor"),
        check_vma=False,
    )
```

```python
import functools

import jax
import jax.numpy as jnp
from jax import lax
from jax.experimental import pallas as pl
from jax.experimental.pallas import tpu as pltpu
from jax.sharding import PartitionSpec as P

adapter_scale = 2.0
MESH = pl.DeviceIdType.MESH


def project_kernel(
    n, per_block, tile, a_ref, w_hbm, o_ref, w_buf, part, from_left, from_right,
    w_sem, left_sem, right_sem, to_right_sem, to_left_sem,
):
    me = lax.axis_index("tensor")
    steps = (n - 1) * per_block
    skew = 2

    def fetch(t):
        return pltpu.make_async_copy(
            w_hbm.at[:, pl.ds(pl.multiple_of(t * tile, tile), tile)], w_buf.at[t], w_sem.at[t]
        )

    def send_right(t):
        return pltpu.make_async_remote_copy(
            src_ref=from_left.at[t], dst_ref=from_left.at[t],
            send_sem=to_right_sem.at[t], recv_sem=left_sem.at[t],
            device_id={"tensor": me + 1}, device_id_type=MESH,
        )

    def send_left(t):
        return pltpu.make_async_remote_copy(
            src_ref=from_right.at[t], dst_ref=from_right.at[t],
            send_sem=to_left_sem.at[t], recv_sem=right_sem.at[t],
            device_id={"tensor": me - 1}, device_id_type=MESH,
        )

    def blocks(i):
        turn, piece = i // per_block, i % per_block
        return n - 1 - turn, turn, piece

    def fetch_step(i, carry):
        right_block, left_block, piece = blocks(i)

        @pl.when(right_block > me)
        def _():
            fetch(right_block * per_block + piece).start()

        @pl.when(left_block < me)
        def _():
            fetch(left_block * per_block + piece).start()

        return carry

    def fetch_own(i, carry):
        fetch(me * per_block + i).start()
        return carry

    lax.fori_loop(0, steps, fetch_step, 0)
    lax.fori_loop(0, per_block, fetch_own, 0)

    barrier = pltpu.get_barrier_semaphore()

    @pl.when(me > 0)
    def _():
        pl.semaphore_signal(barrier, inc=1, device_id={"tensor": me - 1}, device_id_type=MESH)

    @pl.when(me < n - 1)
    def _():
        pl.semaphore_signal(barrier, inc=1, device_id={"tensor": me + 1}, device_id_type=MESH)

    peers = (me > 0).astype(jnp.int32) + (me < n - 1).astype(jnp.int32)
    pl.semaphore_wait(barrier, peers)

    def product(t):
        fetch(t).wait()
        part[...] = jnp.dot(a_ref[...], w_buf[t], preferred_element_type=jnp.float32)

    def step(turn, carry):
        going_right, going_left = turn - me * skew, turn - (n - 1 - me) * skew
        i = lax.max(going_right, 0)
        block, piece = n - 1 - i // per_block, i % per_block

        @pl.when((going_right >= 0) & (going_right < steps) & (block > me))
        def _():
            t = block * per_block + piece
            product(t)

            @pl.when(me > 0)
            def _():
                send_right(t).wait_recv()
                part[...] += from_left[t].astype(jnp.float32)

            from_left[t] = part[...].astype(jnp.bfloat16)
            send_right(t).start()

        k = lax.max(going_left, 0)
        other, piece_left = k // per_block, k % per_block

        @pl.when((going_left >= 0) & (going_left < steps) & (other < me))
        def _():
            t = other * per_block + piece_left
            product(t)

            @pl.when(me < n - 1)
            def _():
                send_left(t).wait_recv()
                part[...] += from_right[t].astype(jnp.float32)

            from_right[t] = part[...].astype(jnp.bfloat16)
            send_left(t).start()

        return carry

    lax.fori_loop(0, steps + (n - 1) * skew, step, 0)

    def own(i, carry):
        t = me * per_block + i
        product(t)

        @pl.when(me > 0)
        def _():
            send_right(t).wait_recv()
            part[...] += from_left[t].astype(jnp.float32)

        @pl.when(me < n - 1)
        def _():
            send_left(t).wait_recv()
            part[...] += from_right[t].astype(jnp.float32)

        o_ref[:, pl.ds(pl.multiple_of(i * tile, tile), tile)] = part[...]
        return carry

    lax.fori_loop(0, per_block, own, 0)

    def drain(i, carry):
        right_block, left_block, piece = blocks(i)

        @pl.when(right_block > me)
        def _():
            send_right(right_block * per_block + piece).wait_send()

        @pl.when(left_block < me)
        def _():
            send_left(left_block * per_block + piece).wait_send()

        return carry

    lax.fori_loop(0, steps, drain, 0)


def project(inputs, weight, n, at, rows, collective_id):
    depth = inputs.shape[1]
    columns = weight.shape[1]
    width = columns // n
    tile = min(256, width)
    per_block = width // tile
    tiles = n * per_block
    return pl.pallas_call(
        functools.partial(project_kernel, n, per_block, tile),
        out_shape=jax.ShapeDtypeStruct((rows, width), jnp.float32),
        grid=(1,),
        in_specs=[
            pl.BlockSpec((rows, depth), lambda _: (at, 0), pipeline_mode=pl.Buffered(1)),
            pl.BlockSpec(memory_space=pl.ANY),
        ],
        out_specs=pl.BlockSpec((rows, width), lambda _: (0, 0), pipeline_mode=pl.Buffered(1)),
        scratch_shapes=[
            pltpu.VMEM((tiles, depth, tile), jnp.bfloat16),
            pltpu.VMEM((rows, tile), jnp.float32),
            pltpu.VMEM((tiles, rows, tile), jnp.bfloat16),
            pltpu.VMEM((tiles, rows, tile), jnp.bfloat16),
            pltpu.SemaphoreType.DMA((tiles,)),
            pltpu.SemaphoreType.DMA((tiles,)),
            pltpu.SemaphoreType.DMA((tiles,)),
            pltpu.SemaphoreType.DMA((tiles,)),
            pltpu.SemaphoreType.DMA((tiles,)),
        ],
        compiler_params=pltpu.CompilerParams(
            collective_id=collective_id, has_side_effects=True, vmem_limit_bytes=60 * 2**20
        ),
        cost_estimate=pl.CostEstimate(
            flops=2 * rows * depth * columns,
            bytes_accessed=2 * depth * columns + 64 * rows * width,
            transcendentals=0,
        ),
    )(inputs, weight)


def owned(slots_ref, columns, rank):
    column = lax.broadcasted_iota(jnp.int32, (1, columns), 1)
    mine = slots_ref[0] == column // rank
    pick = lax.broadcasted_iota(jnp.int32, (rank, columns), 0) == column % rank
    return mine, pick.astype(jnp.bfloat16)


def shrink_kernel(wanted, inputs_ref, slots_ref, *refs):
    maps, out_ref = refs[:-1], refs[-1]
    rank = out_ref.shape[1]
    mine, pick = owned(slots_ref, len(maps) * rank, rank)
    down = jnp.concatenate([m[0] for m in maps], axis=0)
    every = lax.dot_general(
        inputs_ref[0], down, (((1,), (1,)), ((), ())), preferred_element_type=jnp.float32
    )
    masked = jnp.where(mine, every, 0.0).astype(jnp.bfloat16)
    out_ref[0] = lax.dot_general(
        pick, masked, (((1,), (1,)), ((), ())), preferred_element_type=jnp.float32
    ).astype(jnp.bfloat16)


def expand_kernel(wanted, shrink_ref, slots_ref, *refs):
    maps, out_ref = refs[:-1], refs[-1]
    rank = shrink_ref.shape[1]
    mine, pick = owned(slots_ref, len(maps) * rank, rank)
    spread = lax.dot_general(
        shrink_ref[0], pick, (((0,), (0,)), ((), ())), preferred_element_type=jnp.float32
    )
    spread = jnp.where(mine, spread, 0.0).astype(jnp.bfloat16)
    up = jnp.concatenate([m[0] for m in maps], axis=0)
    out_ref[0] = jnp.dot(spread, up, preferred_element_type=jnp.float32).astype(jnp.bfloat16)


def with_adapters(kernel, wanted, operand, slots, maps, out_shape):
    count, per_owner = wanted.shape
    rank, width = maps.shape[1:]

    def adapter(j):
        return pl.BlockSpec((1, rank, width), lambda i, w: (w[i, j], 0, 0))

    def whole(shape):
        return pl.BlockSpec((1,) + shape[1:], lambda i, w: (i, 0, 0))

    return pl.pallas_call(
        kernel,
        out_shape=jax.ShapeDtypeStruct(out_shape, jnp.bfloat16),
        grid_spec=pltpu.PrefetchScalarGridSpec(
            num_scalar_prefetch=1,
            grid=(count,),
            in_specs=[whole(operand.shape), whole(slots.shape)]
            + [adapter(j) for j in range(per_owner)],
            out_specs=whole(out_shape),
        ),
        compiler_params=pltpu.CompilerParams(vmem_limit_bytes=48 * 2**20),
    )(wanted, operand, slots, *([maps] * per_owner))


def shards(
    groups,
    n,
    attention,
    residual,
    output_weight,
    adapter_down_maps,
    adapter_up_maps,
    lacking_adapter_lists,
    request_slot_index,
):
    step_count, row_count, feature_count = attention.shape
    rank = adapter_down_maps.shape[1]
    width = residual.shape[2]
    owners, per_owner = lacking_adapter_lists.shape[2:]
    me = lax.axis_index("dp")
    batches = groups * step_count
    rows = step_count * row_count

    everyone = lax.all_gather(attention, "dp", axis=0)
    small = jnp.concatenate(
        [lacking_adapter_lists[:, 0].reshape(step_count, -1), request_slot_index], axis=1
    )
    small = lax.all_gather(small, "dp", axis=0)
    wanted = small[:, :, : owners * per_owner].reshape(batches, owners, per_owner)
    wanted = lax.dynamic_index_in_dim(wanted, me, axis=1, keepdims=False)
    slots = small[:, :, owners * per_owner :] - me * per_owner
    slots = slots.reshape(batches, row_count, 1)

    flat = attention.reshape(rows, feature_count)
    first = project(flat, output_weight, n, 0, rows // 3, 1)
    everyone, first = lax.optimization_barrier((everyone, first))
    shrink = with_adapters(
        shrink_kernel, wanted, everyone.reshape(batches, row_count, feature_count), slots,
        adapter_down_maps, (batches, rank, row_count),
    )

    shrink, flat = lax.optimization_barrier((shrink, flat))
    second = project(flat, output_weight, n, 2, rows // 6, 2)
    total = lax.psum(shrink, "tensor")
    total, second = lax.optimization_barrier((total, second))
    lora = with_adapters(
        expand_kernel, wanted, total, slots, adapter_up_maps, (batches, row_count, width)
    )

    lora, flat = lax.optimization_barrier((lora, flat))
    third = project(flat, output_weight, n, 1, rows // 2, 3)
    lora_own = lax.psum_scatter(
        lora.reshape(groups, rows, width), "dp", scatter_dimension=0, tiled=False
    )
    projected = jnp.concatenate([first, second, third], axis=0)
    mixed = (
        residual.reshape(rows, width).astype(jnp.float32)
        + projected
        + adapter_scale * lora_own.astype(jnp.float32)
    )
    return mixed.astype(jnp.bfloat16).reshape(residual.shape)


def solution(mesh):
    placed = (
        P(None, ("rep", "dp"), "tensor"),
        P(None, ("rep", "dp"), "tensor"),
        P("tensor", None),
        P("dp", None, "tensor"),
        P("dp", None, "tensor"),
        P(None, ("rep", "dp"), None, None),
        P(None, ("rep", "dp")),
    )
    return jax.shard_map(
        functools.partial(shards, mesh.shape["dp"], mesh.shape["tensor"]),
        mesh=mesh,
        in_specs=placed,
        out_specs=P(None, ("rep", "dp"), "tensor"),
        check_vma=False,
    )
```

```python
import functools

import jax
import jax.numpy as jnp
from jax import lax
from jax.experimental import pallas as pl
from jax.experimental.pallas import tpu as pltpu
from jax.sharding import PartitionSpec as P

adapter_scale = 2.0
MESH = pl.DeviceIdType.MESH


def project_kernel(
    n, per_block, tile, a_ref, w_hbm, o_ref, w_buf, part, from_left, from_right,
    w_sem, left_sem, right_sem, to_right_sem, to_left_sem,
):
    me = lax.axis_index("tensor")
    steps = (n - 1) * per_block
    skew, ahead = 2, 3
    turns = steps + (n - 1) * skew

    def fetch(t):
        return pltpu.make_async_copy(
            w_hbm.at[:, pl.ds(pl.multiple_of(t * tile, tile), tile)], w_buf.at[t], w_sem.at[t]
        )

    def send_right(t):
        return pltpu.make_async_remote_copy(
            src_ref=from_left.at[t], dst_ref=from_left.at[t],
            send_sem=to_right_sem.at[t], recv_sem=left_sem.at[t],
            device_id={"tensor": me + 1}, device_id_type=MESH,
        )

    def send_left(t):
        return pltpu.make_async_remote_copy(
            src_ref=from_right.at[t], dst_ref=from_right.at[t],
            send_sem=to_left_sem.at[t], recv_sem=right_sem.at[t],
            device_id={"tensor": me - 1}, device_id_type=MESH,
        )

    def right_flow(turn):
        going = turn - me * skew
        i = lax.max(going, 0)
        block = n - 1 - i // per_block
        return (going >= 0) & (going < steps) & (block > me), block * per_block + i % per_block

    def left_flow(turn):
        going = turn - (n - 1 - me) * skew
        i = lax.max(going, 0)
        return (going >= 0) & (going < steps) & (i // per_block < me), i

    def fetch_turn(turn, carry):
        for flow in (right_flow, left_flow):
            active, t = flow(turn)

            @pl.when(active)
            def _():
                fetch(t).start()

        return carry

    lax.fori_loop(0, ahead, fetch_turn, 0)

    barrier = pltpu.get_barrier_semaphore()

    @pl.when(me > 0)
    def _():
        pl.semaphore_signal(barrier, inc=1, device_id={"tensor": me - 1}, device_id_type=MESH)

    @pl.when(me < n - 1)
    def _():
        pl.semaphore_signal(barrier, inc=1, device_id={"tensor": me + 1}, device_id_type=MESH)

    peers = (me > 0).astype(jnp.int32) + (me < n - 1).astype(jnp.int32)
    pl.semaphore_wait(barrier, peers)

    def product(t):
        fetch(t).wait()
        part[...] = jnp.dot(a_ref[...], w_buf[t], preferred_element_type=jnp.float32)

    def step(turn, carry):
        fetch_turn(turn + ahead, 0)

        @pl.when(turn < per_block)
        def _():
            fetch(me * per_block + turn).start()

        active, t = right_flow(turn)

        @pl.when(active)
        def _():
            product(t)

            @pl.when(me > 0)
            def _():
                send_right(t).wait_recv()
                part[...] += from_left[t].astype(jnp.float32)

            from_left[t] = part[...].astype(jnp.bfloat16)
            send_right(t).start()

        other, u = left_flow(turn)

        @pl.when(other)
        def _():
            product(u)

            @pl.when(me < n - 1)
            def _():
                send_left(u).wait_recv()
                part[...] += from_right[u].astype(jnp.float32)

            from_right[u] = part[...].astype(jnp.bfloat16)
            send_left(u).start()

        return carry

    lax.fori_loop(0, turns, step, 0)

    def own(i, carry):
        t = me * per_block + i
        product(t)

        @pl.when(me > 0)
        def _():
            send_right(t).wait_recv()
            part[...] += from_left[t].astype(jnp.float32)

        @pl.when(me < n - 1)
        def _():
            send_left(t).wait_recv()
            part[...] += from_right[t].astype(jnp.float32)

        o_ref[:, pl.ds(pl.multiple_of(i * tile, tile), tile)] = part[...]
        return carry

    lax.fori_loop(0, per_block, own, 0)

    def drain(turn, carry):
        active, t = right_flow(turn)

        @pl.when(active)
        def _():
            send_right(t).wait_send()

        other, u = left_flow(turn)

        @pl.when(other)
        def _():
            send_left(u).wait_send()

        return carry

    lax.fori_loop(0, turns, drain, 0)


def project(inputs, weight, n, at, rows, collective_id):
    depth = inputs.shape[1]
    columns = weight.shape[1]
    width = columns // n
    tile = min(256, width)
    per_block = width // tile
    tiles = n * per_block
    return pl.pallas_call(
        functools.partial(project_kernel, n, per_block, tile),
        out_shape=jax.ShapeDtypeStruct((rows, width), jnp.float32),
        grid=(1,),
        in_specs=[
            pl.BlockSpec((rows, depth), lambda _: (at, 0), pipeline_mode=pl.Buffered(1)),
            pl.BlockSpec(memory_space=pl.ANY),
        ],
        out_specs=pl.BlockSpec((rows, width), lambda _: (0, 0), pipeline_mode=pl.Buffered(1)),
        scratch_shapes=[
            pltpu.VMEM((tiles, depth, tile), jnp.bfloat16),
            pltpu.VMEM((rows, tile), jnp.float32),
            pltpu.VMEM((tiles, rows, tile), jnp.bfloat16),
            pltpu.VMEM((tiles, rows, tile), jnp.bfloat16),
            pltpu.SemaphoreType.DMA((tiles,)),
            pltpu.SemaphoreType.DMA((tiles,)),
            pltpu.SemaphoreType.DMA((tiles,)),
            pltpu.SemaphoreType.DMA((tiles,)),
            pltpu.SemaphoreType.DMA((tiles,)),
        ],
        compiler_params=pltpu.CompilerParams(
            collective_id=collective_id, has_side_effects=True, vmem_limit_bytes=60 * 2**20
        ),
        cost_estimate=pl.CostEstimate(
            flops=2 * rows * depth * columns,
            bytes_accessed=2 * depth * columns + 64 * rows * width,
            transcendentals=0,
        ),
    )(inputs, weight)


def owned(slots_ref, columns, rank):
    column = lax.broadcasted_iota(jnp.int32, (1, columns), 1)
    mine = slots_ref[0] == column // rank
    pick = lax.broadcasted_iota(jnp.int32, (rank, columns), 0) == column % rank
    return mine, pick.astype(jnp.bfloat16)


def fetched(wanted, maps_hbm, held, sems):
    i, count = pl.program_id(0), pl.num_programs(0)
    slots, rank = held.shape[0], maps_hbm.shape[1]

    def copies(step):
        slot = lax.rem(step, slots)
        return [
            pltpu.make_async_copy(
                maps_hbm.at[wanted[step, j]], held.at[slot, pl.ds(j * rank, rank)], sems.at[slot, j]
            )
            for j in range(wanted.shape[1])
        ]

    @pl.when(i == 0)
    def _():
        for step in range(slots - 1):
            for copy in copies(step):
                copy.start()

    @pl.when(i + slots - 1 < count)
    def _():
        for copy in copies(i + slots - 1):
            copy.start()

    for copy in copies(i):
        copy.wait()
    return held[lax.rem(i, slots)]


def shrink_kernel(wanted, inputs_ref, slots_ref, maps_hbm, out_ref, held, sems):
    mine, pick = owned(slots_ref, held.shape[1], out_ref.shape[1])
    down = fetched(wanted, maps_hbm, held, sems)
    every = lax.dot_general(
        inputs_ref[0], down, (((1,), (1,)), ((), ())), preferred_element_type=jnp.float32
    )
    masked = jnp.where(mine, every, 0.0).astype(jnp.bfloat16)
    out_ref[0] = lax.dot_general(
        pick, masked, (((1,), (1,)), ((), ())), preferred_element_type=jnp.float32
    ).astype(jnp.bfloat16)


def expand_kernel(wanted, shrink_ref, slots_ref, maps_hbm, out_ref, held, sems):
    mine, pick = owned(slots_ref, held.shape[1], shrink_ref.shape[1])
    spread = lax.dot_general(
        shrink_ref[0], pick, (((0,), (0,)), ((), ())), preferred_element_type=jnp.float32
    )
    spread = jnp.where(mine, spread, 0.0).astype(jnp.bfloat16)
    up = fetched(wanted, maps_hbm, held, sems)
    out_ref[0] = jnp.dot(spread, up, preferred_element_type=jnp.float32).astype(jnp.bfloat16)


def with_adapters(kernel, wanted, operand, slots, maps, out_shape):
    count, per_owner = wanted.shape
    rank, width = maps.shape[1:]
    depth = min(4, count)

    def whole(shape):
        return pl.BlockSpec((1,) + shape[1:], lambda i, w: (i, 0, 0))

    return pl.pallas_call(
        kernel,
        out_shape=jax.ShapeDtypeStruct(out_shape, jnp.bfloat16),
        grid_spec=pltpu.PrefetchScalarGridSpec(
            num_scalar_prefetch=1,
            grid=(count,),
            in_specs=[
                whole(operand.shape), whole(slots.shape), pl.BlockSpec(memory_space=pl.ANY),
            ],
            out_specs=whole(out_shape),
            scratch_shapes=[
                pltpu.VMEM((depth, per_owner * rank, width), jnp.bfloat16),
                pltpu.SemaphoreType.DMA((depth, per_owner)),
            ],
        ),
        compiler_params=pltpu.CompilerParams(vmem_limit_bytes=48 * 2**20),
    )(wanted, operand, slots, maps)


def mix_kernel(residual_ref, lora_ref, first_ref, second_ref, third_ref, out_ref):
    i = pl.program_id(0)

    def mix(projected_ref):
        out_ref[...] = (
            residual_ref[...].astype(jnp.float32)
            + projected_ref[...]
            + adapter_scale * lora_ref[...].astype(jnp.float32)
        ).astype(jnp.bfloat16)

    pl.when(i < 2)(lambda: mix(first_ref))
    pl.when(i == 2)(lambda: mix(second_ref))
    pl.when(i > 2)(lambda: mix(third_ref))


def mix(residual, lora, first, second, third):
    rows, width = residual.shape
    block = (rows // 6, width)
    return pl.pallas_call(
        mix_kernel,
        out_shape=jax.ShapeDtypeStruct((rows, width), jnp.bfloat16),
        grid=(6,),
        in_specs=[
            pl.BlockSpec(block, lambda i: (i, 0)),
            pl.BlockSpec(block, lambda i: (i, 0)),
            pl.BlockSpec(block, lambda i: (jnp.minimum(i, 1), 0)),
            pl.BlockSpec(block, lambda i: (0, 0)),
            pl.BlockSpec(block, lambda i: (jnp.maximum(i - 3, 0), 0)),
        ],
        out_specs=pl.BlockSpec(block, lambda i: (i, 0)),
        compiler_params=pltpu.CompilerParams(vmem_limit_bytes=48 * 2**20),
    )(residual, lora, first, second, third)


def shards(
    groups,
    n,
    attention,
    residual,
    output_weight,
    adapter_down_maps,
    adapter_up_maps,
    lacking_adapter_lists,
    request_slot_index,
):
    step_count, row_count, feature_count = attention.shape
    rank = adapter_down_maps.shape[1]
    width = residual.shape[2]
    owners, per_owner = lacking_adapter_lists.shape[2:]
    me = lax.axis_index("dp")
    batches = groups * step_count
    rows = step_count * row_count

    everyone = lax.all_gather(attention, "dp", axis=0)
    small = jnp.concatenate(
        [lacking_adapter_lists[:, 0].reshape(step_count, -1), request_slot_index], axis=1
    )
    group = jnp.arange(groups, dtype=jnp.int32)[:, None, None]
    gathered = jnp.where(group == me, small[None], 0)
    for shift in range(1, groups):
        ring = [(i, (i + shift) % groups) for i in range(groups)]
        passed = lax.ppermute(small, "dp", ring)
        gathered = jnp.where(group == (me + groups - shift) % groups, passed[None], gathered)
    small = gathered
    wanted = small[:, :, : owners * per_owner].reshape(batches, owners, per_owner)
    wanted = lax.dynamic_index_in_dim(wanted, me, axis=1, keepdims=False)
    slots = small[:, :, owners * per_owner :] - me * per_owner
    slots = slots.reshape(batches, row_count, 1)

    flat = attention.reshape(rows, feature_count)
    first = project(flat, output_weight, n, 0, rows // 3, 1)
    everyone, first = lax.optimization_barrier((everyone, first))
    shrink = with_adapters(
        shrink_kernel, wanted, everyone.reshape(batches, row_count, feature_count), slots,
        adapter_down_maps, (batches, rank, row_count),
    )

    shrink, flat = lax.optimization_barrier((shrink, flat))
    second = project(flat, output_weight, n, 2, rows // 6, 2)
    total = lax.psum(shrink, "tensor")
    total, second = lax.optimization_barrier((total, second))
    lora = with_adapters(
        expand_kernel, wanted, total, slots, adapter_up_maps, (batches, row_count, width)
    )

    lora, flat = lax.optimization_barrier((lora, flat))
    third = project(flat, output_weight, n, 1, rows // 2, 3)
    lora_own = lax.psum_scatter(
        lora.reshape(groups, rows, width), "dp", scatter_dimension=0, tiled=False
    )
    mixed = mix(residual.reshape(rows, width), lora_own, first, second, third)
    return mixed.reshape(residual.shape)


def solution(mesh):
    placed = (
        P(None, ("rep", "dp"), "tensor"),
        P(None, ("rep", "dp"), "tensor"),
        P("tensor", None),
        P("dp", None, "tensor"),
        P("dp", None, "tensor"),
        P(None, ("rep", "dp"), None, None),
        P(None, ("rep", "dp")),
    )
    return jax.shard_map(
        functools.partial(shards, mesh.shape["dp"], mesh.shape["tensor"]),
        mesh=mesh,
        in_specs=placed,
        out_specs=P(None, ("rep", "dp"), "tensor"),
        check_vma=False,
    )
```

```python
import functools
import math

import jax
import jax.numpy as jnp
from jax import lax
from jax.experimental import pallas as pl
from jax.experimental.pallas import tpu as pltpu
from jax.sharding import PartitionSpec as P

adapter_scale = 2.0
MESH = pl.DeviceIdType.MESH


def project_kernel(
    n, per_block, tile, start, a_hbm, w_hbm, o_ref, a_ref, w_buf, part, from_left, from_right,
    a_sem, w_sem, left_sem, right_sem, to_right_sem, to_left_sem,
):
    me = lax.axis_index("tensor")
    steps = (n - 1) * per_block
    skew, ahead = 2, 3
    turns = steps + (n - 1) * skew

    def fetch(t):
        return pltpu.make_async_copy(
            w_hbm.at[:, pl.ds(pl.multiple_of(t * tile, tile), tile)], w_buf.at[t], w_sem.at[t]
        )

    def send_right(t):
        return pltpu.make_async_remote_copy(
            src_ref=from_left.at[t], dst_ref=from_left.at[t],
            send_sem=to_right_sem.at[t], recv_sem=left_sem.at[t],
            device_id={"tensor": me + 1}, device_id_type=MESH,
        )

    def send_left(t):
        return pltpu.make_async_remote_copy(
            src_ref=from_right.at[t], dst_ref=from_right.at[t],
            send_sem=to_left_sem.at[t], recv_sem=right_sem.at[t],
            device_id={"tensor": me - 1}, device_id_type=MESH,
        )

    def right_flow(turn):
        going = turn - me * skew
        i = lax.max(going, 0)
        block = n - 1 - i // per_block
        return (going >= 0) & (going < steps) & (block > me), block * per_block + i % per_block

    def left_flow(turn):
        going = turn - (n - 1 - me) * skew
        i = lax.max(going, 0)
        return (going >= 0) & (going < steps) & (i // per_block < me), i

    def fetch_turn(turn, carry):
        for flow in (right_flow, left_flow):
            active, t = flow(turn)

            @pl.when(active)
            def _():
                fetch(t).start()

        return carry

    inputs = pltpu.make_async_copy(a_hbm.at[pl.ds(start, a_ref.shape[0])], a_ref, a_sem)
    inputs.start()
    lax.fori_loop(0, ahead, fetch_turn, 0)

    barrier = pltpu.get_barrier_semaphore()

    @pl.when(me > 0)
    def _():
        pl.semaphore_signal(barrier, inc=1, device_id={"tensor": me - 1}, device_id_type=MESH)

    @pl.when(me < n - 1)
    def _():
        pl.semaphore_signal(barrier, inc=1, device_id={"tensor": me + 1}, device_id_type=MESH)

    peers = (me > 0).astype(jnp.int32) + (me < n - 1).astype(jnp.int32)
    pl.semaphore_wait(barrier, peers)
    inputs.wait()

    def product(t):
        fetch(t).wait()
        part[...] = jnp.dot(a_ref[...], w_buf[t], preferred_element_type=jnp.float32)

    def step(turn, carry):
        fetch_turn(turn + ahead, 0)

        @pl.when(turn < per_block)
        def _():
            fetch(me * per_block + turn).start()

        active, t = right_flow(turn)

        @pl.when(active)
        def _():
            product(t)

            @pl.when(me > 0)
            def _():
                send_right(t).wait_recv()
                part[...] += from_left[t].astype(jnp.float32)

            from_left[t] = part[...].astype(jnp.bfloat16)
            send_right(t).start()

        other, u = left_flow(turn)

        @pl.when(other)
        def _():
            product(u)

            @pl.when(me < n - 1)
            def _():
                send_left(u).wait_recv()
                part[...] += from_right[u].astype(jnp.float32)

            from_right[u] = part[...].astype(jnp.bfloat16)
            send_left(u).start()

        return carry

    lax.fori_loop(0, turns, step, 0)

    def own(i, carry):
        t = me * per_block + i
        product(t)

        @pl.when(me > 0)
        def _():
            send_right(t).wait_recv()
            part[...] += from_left[t].astype(jnp.float32)

        @pl.when(me < n - 1)
        def _():
            send_left(t).wait_recv()
            part[...] += from_right[t].astype(jnp.float32)

        o_ref[:, pl.ds(pl.multiple_of(i * tile, tile), tile)] = part[...]
        return carry

    lax.fori_loop(0, per_block, own, 0)

    def drain(turn, carry):
        active, t = right_flow(turn)

        @pl.when(active)
        def _():
            send_right(t).wait_send()

        other, u = left_flow(turn)

        @pl.when(other)
        def _():
            send_left(u).wait_send()

        return carry

    lax.fori_loop(0, turns, drain, 0)


def project(inputs, weight, n, start, rows, collective_id):
    depth = inputs.shape[1]
    columns = weight.shape[1]
    width = columns // n
    tile = min(256, width)
    per_block = width // tile
    tiles = n * per_block
    return pl.pallas_call(
        functools.partial(project_kernel, n, per_block, tile, start),
        out_shape=jax.ShapeDtypeStruct((rows, width), jnp.float32),
        in_specs=[pl.BlockSpec(memory_space=pl.ANY)] * 2,
        out_specs=pl.BlockSpec(memory_space=pltpu.VMEM),
        scratch_shapes=[
            pltpu.VMEM((rows, depth), jnp.bfloat16),
            pltpu.VMEM((tiles, depth, tile), jnp.bfloat16),
            pltpu.VMEM((rows, tile), jnp.float32),
            pltpu.VMEM((tiles, rows, tile), jnp.bfloat16),
            pltpu.VMEM((tiles, rows, tile), jnp.bfloat16),
            pltpu.SemaphoreType.DMA,
            pltpu.SemaphoreType.DMA((tiles,)),
            pltpu.SemaphoreType.DMA((tiles,)),
            pltpu.SemaphoreType.DMA((tiles,)),
            pltpu.SemaphoreType.DMA((tiles,)),
            pltpu.SemaphoreType.DMA((tiles,)),
        ],
        compiler_params=pltpu.CompilerParams(
            collective_id=collective_id, has_side_effects=True, vmem_limit_bytes=60 * 2**20
        ),
        cost_estimate=pl.CostEstimate(
            flops=2 * rows * depth * columns,
            bytes_accessed=2 * depth * columns + 64 * rows * width,
            transcendentals=0,
        ),
    )(inputs, weight)


def owned(slots_ref, columns, rank):
    column = lax.broadcasted_iota(jnp.int32, (1, columns), 1)
    mine = slots_ref[0] == column // rank
    pick = lax.broadcasted_iota(jnp.int32, (rank, columns), 0) == column % rank
    return mine, pick.astype(jnp.bfloat16)


def fetched(wanted, maps_hbm, held, sems):
    i, count = pl.program_id(0), pl.num_programs(0)
    slots, rank = held.shape[0], maps_hbm.shape[1]

    def copies(step):
        slot = lax.rem(step, slots)
        return [
            pltpu.make_async_copy(
                maps_hbm.at[wanted[step, j]], held.at[slot, pl.ds(j * rank, rank)], sems.at[slot, j]
            )
            for j in range(wanted.shape[1])
        ]

    @pl.when(i == 0)
    def _():
        for step in range(slots - 1):
            for copy in copies(step):
                copy.start()

    @pl.when(i + slots - 1 < count)
    def _():
        for copy in copies(i + slots - 1):
            copy.start()

    for copy in copies(i):
        copy.wait()
    return held[lax.rem(i, slots)]


def shrink_kernel(wanted, inputs_ref, slots_ref, maps_hbm, out_ref, held, sems):
    mine, pick = owned(slots_ref, held.shape[1], out_ref.shape[1])
    down = fetched(wanted, maps_hbm, held, sems)
    every = lax.dot_general(
        inputs_ref[0], down, (((1,), (1,)), ((), ())), preferred_element_type=jnp.float32
    )
    masked = jnp.where(mine, every, 0.0).astype(jnp.bfloat16)
    out_ref[0] = lax.dot_general(
        pick, masked, (((1,), (1,)), ((), ())), preferred_element_type=jnp.float32
    ).astype(jnp.bfloat16)


def expand_kernel(wanted, shrink_ref, slots_ref, maps_hbm, out_ref, held, sems):
    mine, pick = owned(slots_ref, held.shape[1], shrink_ref.shape[1])
    spread = lax.dot_general(
        shrink_ref[0], pick, (((0,), (0,)), ((), ())), preferred_element_type=jnp.float32
    )
    spread = jnp.where(mine, spread, 0.0).astype(jnp.bfloat16)
    up = fetched(wanted, maps_hbm, held, sems)
    out_ref[0] = jnp.dot(spread, up, preferred_element_type=jnp.float32).astype(jnp.bfloat16)


def with_adapters(kernel, wanted, operand, slots, maps, out_shape):
    count, per_owner = wanted.shape
    rank, width = maps.shape[1:]
    depth = min(4, count)

    def whole(shape):
        return pl.BlockSpec((1,) + shape[1:], lambda i, w: (i, 0, 0))

    return pl.pallas_call(
        kernel,
        out_shape=jax.ShapeDtypeStruct(out_shape, jnp.bfloat16),
        grid_spec=pltpu.PrefetchScalarGridSpec(
            num_scalar_prefetch=1,
            grid=(count,),
            in_specs=[
                whole(operand.shape), whole(slots.shape), pl.BlockSpec(memory_space=pl.ANY),
            ],
            out_specs=whole(out_shape),
            scratch_shapes=[
                pltpu.VMEM((depth, per_owner * rank, width), jnp.bfloat16),
                pltpu.SemaphoreType.DMA((depth, per_owner)),
            ],
        ),
        compiler_params=pltpu.CompilerParams(vmem_limit_bytes=48 * 2**20),
    )(wanted, operand, slots, maps)


def mix_kernel(ends, residual_ref, lora_ref, first_ref, second_ref, third_ref, out_ref):
    i = pl.program_id(0)

    def mix(projected_ref):
        out_ref[...] = (
            residual_ref[...].astype(jnp.float32)
            + projected_ref[...]
            + adapter_scale * lora_ref[...].astype(jnp.float32)
        ).astype(jnp.bfloat16)

    pl.when(i < ends[0])(lambda: mix(first_ref))
    pl.when((i >= ends[0]) & (i < ends[1]))(lambda: mix(second_ref))
    pl.when(i >= ends[1])(lambda: mix(third_ref))


def mix(residual, lora, *pieces):
    rows, width = residual.shape
    size = math.gcd(*(piece.shape[0] for piece in pieces))
    block = (size, width)
    counts = [piece.shape[0] // size for piece in pieces]
    starts = [0, counts[0], counts[0] + counts[1]]

    def of_piece(start, count):
        return pl.BlockSpec(block, lambda i: (jnp.clip(i - start, 0, count - 1), 0))

    return pl.pallas_call(
        functools.partial(mix_kernel, starts[1:]),
        out_shape=jax.ShapeDtypeStruct((rows, width), jnp.bfloat16),
        grid=(rows // size,),
        in_specs=[pl.BlockSpec(block, lambda i: (i, 0))] * 2
        + [of_piece(start, count) for start, count in zip(starts, counts)],
        out_specs=pl.BlockSpec(block, lambda i: (i, 0)),
        compiler_params=pltpu.CompilerParams(vmem_limit_bytes=48 * 2**20),
    )(residual, lora, *pieces)


def shards(
    groups,
    n,
    attention,
    residual,
    output_weight,
    adapter_down_maps,
    adapter_up_maps,
    lacking_adapter_lists,
    request_slot_index,
):
    step_count, row_count, feature_count = attention.shape
    rank = adapter_down_maps.shape[1]
    width = residual.shape[2]
    owners, per_owner = lacking_adapter_lists.shape[2:]
    me = lax.axis_index("dp")
    batches = groups * step_count
    rows = step_count * row_count

    everyone = lax.all_gather(attention, "dp", axis=0)
    small = jnp.concatenate(
        [lacking_adapter_lists[:, 0].reshape(step_count, -1), request_slot_index], axis=1
    )
    group = jnp.arange(groups, dtype=jnp.int32)[:, None, None]
    gathered = jnp.where(group == me, small[None], 0)
    for shift in range(1, groups):
        ring = [(i, (i + shift) % groups) for i in range(groups)]
        passed = lax.ppermute(small, "dp", ring)
        gathered = jnp.where(group == (me + groups - shift) % groups, passed[None], gathered)
    small = gathered
    wanted = small[:, :, : owners * per_owner].reshape(batches, owners, per_owner)
    wanted = lax.dynamic_index_in_dim(wanted, me, axis=1, keepdims=False)
    slots = small[:, :, owners * per_owner :] - me * per_owner
    slots = slots.reshape(batches, row_count, 1)

    ends = rows * 3 // 8 // 32 * 32, rows * 13 // 24 // 32 * 32
    flat = attention.reshape(rows, feature_count)
    first = project(flat, output_weight, n, 0, ends[0], 1)
    everyone, first = lax.optimization_barrier((everyone, first))
    shrink = with_adapters(
        shrink_kernel, wanted, everyone.reshape(batches, row_count, feature_count), slots,
        adapter_down_maps, (batches, rank, row_count),
    )

    shrink, flat = lax.optimization_barrier((shrink, flat))
    second = project(flat, output_weight, n, ends[0], ends[1] - ends[0], 2)
    total = lax.psum(shrink, "tensor")
    total, second = lax.optimization_barrier((total, second))
    lora = with_adapters(
        expand_kernel, wanted, total, slots, adapter_up_maps, (batches, row_count, width)
    )

    lora, flat = lax.optimization_barrier((lora, flat))
    third = project(flat, output_weight, n, ends[1], rows - ends[1], 3)
    lora_own = lax.psum_scatter(
        lora.reshape(groups, rows, width), "dp", scatter_dimension=0, tiled=False
    )
    mixed = mix(residual.reshape(rows, width), lora_own, first, second, third)
    return mixed.reshape(residual.shape)


def solution(mesh):
    placed = (
        P(None, ("rep", "dp"), "tensor"),
        P(None, ("rep", "dp"), "tensor"),
        P("tensor", None),
        P("dp", None, "tensor"),
        P("dp", None, "tensor"),
        P(None, ("rep", "dp"), None, None),
        P(None, ("rep", "dp")),
    )
    return jax.shard_map(
        functools.partial(shards, mesh.shape["dp"], mesh.shape["tensor"]),
        mesh=mesh,
        in_specs=placed,
        out_specs=P(None, ("rep", "dp"), "tensor"),
        check_vma=False,
    )
```

```python
import functools

import jax
import jax.numpy as jnp
from jax import lax
from jax.experimental import pallas as pl
from jax.experimental.pallas import tpu as pltpu
from jax.sharding import PartitionSpec as P

adapter_scale = 2.0
MESH = pl.DeviceIdType.MESH


def project_kernel(
    n, per_block, tile, start, a_hbm, w_hbm, o_ref, a_ref, w_buf, part, from_left, from_right,
    a_sem, w_sem, left_sem, right_sem, to_right_sem, to_left_sem,
):
    me = lax.axis_index("tensor")
    steps = (n - 1) * per_block
    skew, ahead = 2, 3
    turns = steps + (n - 1) * skew

    def fetch(t):
        return pltpu.make_async_copy(
            w_hbm.at[:, pl.ds(pl.multiple_of(t * tile, tile), tile)], w_buf.at[t], w_sem.at[t]
        )

    def send_right(t):
        return pltpu.make_async_remote_copy(
            src_ref=from_left.at[t], dst_ref=from_left.at[t],
            send_sem=to_right_sem.at[t], recv_sem=left_sem.at[t],
            device_id={"tensor": me + 1}, device_id_type=MESH,
        )

    def send_left(t):
        return pltpu.make_async_remote_copy(
            src_ref=from_right.at[t], dst_ref=from_right.at[t],
            send_sem=to_left_sem.at[t], recv_sem=right_sem.at[t],
            device_id={"tensor": me - 1}, device_id_type=MESH,
        )

    def right_flow(turn):
        going = turn - me * skew
        i = lax.max(going, 0)
        block = n - 1 - i // per_block
        return (going >= 0) & (going < steps) & (block > me), block * per_block + i % per_block

    def left_flow(turn):
        going = turn - (n - 1 - me) * skew
        i = lax.max(going, 0)
        return (going >= 0) & (going < steps) & (i // per_block < me), i

    def fetch_turn(turn, carry):
        for flow in (right_flow, left_flow):
            active, t = flow(turn)

            @pl.when(active)
            def _():
                fetch(t).start()

        return carry

    inputs = pltpu.make_async_copy(a_hbm.at[pl.ds(start, a_ref.shape[0])], a_ref, a_sem)
    inputs.start()
    lax.fori_loop(0, ahead, fetch_turn, 0)

    barrier = pltpu.get_barrier_semaphore()

    @pl.when(me > 0)
    def _():
        pl.semaphore_signal(barrier, inc=1, device_id={"tensor": me - 1}, device_id_type=MESH)

    @pl.when(me < n - 1)
    def _():
        pl.semaphore_signal(barrier, inc=1, device_id={"tensor": me + 1}, device_id_type=MESH)

    peers = (me > 0).astype(jnp.int32) + (me < n - 1).astype(jnp.int32)
    pl.semaphore_wait(barrier, peers)
    inputs.wait()

    def product(t):
        fetch(t).wait()
        part[...] = jnp.dot(a_ref[...], w_buf[t], preferred_element_type=jnp.float32)

    def step(turn, carry):
        fetch_turn(turn + ahead, 0)

        @pl.when(turn < per_block)
        def _():
            fetch(me * per_block + turn).start()

        active, t = right_flow(turn)

        @pl.when(active)
        def _():
            product(t)

            @pl.when(me > 0)
            def _():
                send_right(t).wait_recv()
                part[...] += from_left[t].astype(jnp.float32)

            from_left[t] = part[...].astype(jnp.bfloat16)
            send_right(t).start()

        other, u = left_flow(turn)

        @pl.when(other)
        def _():
            product(u)

            @pl.when(me < n - 1)
            def _():
                send_left(u).wait_recv()
                part[...] += from_right[u].astype(jnp.float32)

            from_right[u] = part[...].astype(jnp.bfloat16)
            send_left(u).start()

        return carry

    lax.fori_loop(0, turns, step, 0)

    def own(i, carry):
        t = me * per_block + i
        product(t)

        @pl.when(me > 0)
        def _():
            send_right(t).wait_recv()
            part[...] += from_left[t].astype(jnp.float32)

        @pl.when(me < n - 1)
        def _():
            send_left(t).wait_recv()
            part[...] += from_right[t].astype(jnp.float32)

        o_ref[:, pl.ds(pl.multiple_of(i * tile, tile), tile)] = part[...]
        return carry

    lax.fori_loop(0, per_block, own, 0)

    def drain(turn, carry):
        active, t = right_flow(turn)

        @pl.when(active)
        def _():
            send_right(t).wait_send()

        other, u = left_flow(turn)

        @pl.when(other)
        def _():
            send_left(u).wait_send()

        return carry

    lax.fori_loop(0, turns, drain, 0)


def project(inputs, weight, n, start, rows, collective_id):
    depth = inputs.shape[1]
    columns = weight.shape[1]
    width = columns // n
    tile = min(256, width)
    per_block = width // tile
    tiles = n * per_block
    return pl.pallas_call(
        functools.partial(project_kernel, n, per_block, tile, start),
        out_shape=jax.ShapeDtypeStruct((rows, width), jnp.float32),
        in_specs=[pl.BlockSpec(memory_space=pl.ANY)] * 2,
        out_specs=pl.BlockSpec(memory_space=pltpu.VMEM),
        scratch_shapes=[
            pltpu.VMEM((rows, depth), jnp.bfloat16),
            pltpu.VMEM((tiles, depth, tile), jnp.bfloat16),
            pltpu.VMEM((rows, tile), jnp.float32),
            pltpu.VMEM((tiles, rows, tile), jnp.bfloat16),
            pltpu.VMEM((tiles, rows, tile), jnp.bfloat16),
            pltpu.SemaphoreType.DMA,
            pltpu.SemaphoreType.DMA((tiles,)),
            pltpu.SemaphoreType.DMA((tiles,)),
            pltpu.SemaphoreType.DMA((tiles,)),
            pltpu.SemaphoreType.DMA((tiles,)),
            pltpu.SemaphoreType.DMA((tiles,)),
        ],
        compiler_params=pltpu.CompilerParams(
            collective_id=collective_id, has_side_effects=True, vmem_limit_bytes=60 * 2**20
        ),
        cost_estimate=pl.CostEstimate(
            flops=2 * rows * depth * columns,
            bytes_accessed=2 * depth * columns + 64 * rows * width,
            transcendentals=0,
        ),
    )(inputs, weight)


def owned(slots_ref, columns, rank):
    column = lax.broadcasted_iota(jnp.int32, (1, columns), 1)
    mine = slots_ref[0] == column // rank
    pick = lax.broadcasted_iota(jnp.int32, (rank, columns), 0) == column % rank
    return mine, pick.astype(jnp.bfloat16)


def fetched(wanted, maps_hbm, held, sems):
    i, count = pl.program_id(0), pl.num_programs(0)
    slots, rank = held.shape[0], maps_hbm.shape[1]

    def copies(step):
        slot = lax.rem(step, slots)
        return [
            pltpu.make_async_copy(
                maps_hbm.at[wanted[step, j]], held.at[slot, pl.ds(j * rank, rank)], sems.at[slot, j]
            )
            for j in range(wanted.shape[1])
        ]

    @pl.when(i == 0)
    def _():
        for step in range(slots - 1):
            for copy in copies(step):
                copy.start()

    @pl.when(i + slots - 1 < count)
    def _():
        for copy in copies(i + slots - 1):
            copy.start()

    for copy in copies(i):
        copy.wait()
    return held[lax.rem(i, slots)]


def shrink_kernel(wanted, inputs_ref, slots_ref, maps_hbm, out_ref, held, sems):
    mine, pick = owned(slots_ref, held.shape[1], out_ref.shape[1])
    down = fetched(wanted, maps_hbm, held, sems)
    every = lax.dot_general(
        inputs_ref[0], down, (((1,), (1,)), ((), ())), preferred_element_type=jnp.float32
    )
    masked = jnp.where(mine, every, 0.0).astype(jnp.bfloat16)
    out_ref[0] = lax.dot_general(
        pick, masked, (((1,), (1,)), ((), ())), preferred_element_type=jnp.float32
    ).astype(jnp.bfloat16)


def expand_kernel(wanted, shrink_ref, slots_ref, maps_hbm, out_ref, held, sems):
    mine, pick = owned(slots_ref, held.shape[1], shrink_ref.shape[1])
    spread = lax.dot_general(
        shrink_ref[0], pick, (((0,), (0,)), ((), ())), preferred_element_type=jnp.float32
    )
    spread = jnp.where(mine, spread, 0.0).astype(jnp.bfloat16)
    up = fetched(wanted, maps_hbm, held, sems)
    out_ref[0] = jnp.dot(spread, up, preferred_element_type=jnp.float32).astype(jnp.bfloat16)


def with_adapters(kernel, wanted, operand, slots, maps, out_shape):
    count, per_owner = wanted.shape
    rank, width = maps.shape[1:]
    depth = min(4, count)

    def whole(shape):
        return pl.BlockSpec((1,) + shape[1:], lambda i, w: (i, 0, 0))

    return pl.pallas_call(
        kernel,
        out_shape=jax.ShapeDtypeStruct(out_shape, jnp.bfloat16),
        grid_spec=pltpu.PrefetchScalarGridSpec(
            num_scalar_prefetch=1,
            grid=(count,),
            in_specs=[
                whole(operand.shape), whole(slots.shape), pl.BlockSpec(memory_space=pl.ANY),
            ],
            out_specs=whole(out_shape),
            scratch_shapes=[
                pltpu.VMEM((depth, per_owner * rank, width), jnp.bfloat16),
                pltpu.SemaphoreType.DMA((depth, per_owner)),
            ],
        ),
        compiler_params=pltpu.CompilerParams(vmem_limit_bytes=48 * 2**20),
    )(wanted, operand, slots, maps)


def mix_kernel(residual_ref, lora_ref, *refs):
    pieces, out_ref = refs[:-1], refs[-1]
    start = 0
    for piece in pieces:
        here = pl.ds(start, piece.shape[0])
        out_ref[here] = (
            residual_ref[here].astype(jnp.float32)
            + piece[...]
            + adapter_scale * lora_ref[here].astype(jnp.float32)
        ).astype(jnp.bfloat16)
        start += piece.shape[0]


def mix(residual, lora, *pieces):
    rows, width = residual.shape
    tile = min(256, width)

    def columns(array):
        return pl.BlockSpec((array.shape[0], tile), lambda i: (0, i))

    return pl.pallas_call(
        mix_kernel,
        out_shape=jax.ShapeDtypeStruct((rows, width), jnp.bfloat16),
        grid=(width // tile,),
        in_specs=[columns(array) for array in (residual, lora, *pieces)],
        out_specs=columns(residual),
        compiler_params=pltpu.CompilerParams(vmem_limit_bytes=48 * 2**20),
    )(residual, lora, *pieces)


def shards(
    groups,
    n,
    attention,
    residual,
    output_weight,
    adapter_down_maps,
    adapter_up_maps,
    lacking_adapter_lists,
    request_slot_index,
):
    step_count, row_count, feature_count = attention.shape
    rank = adapter_down_maps.shape[1]
    width = residual.shape[2]
    owners, per_owner = lacking_adapter_lists.shape[2:]
    me = lax.axis_index("dp")
    batches = groups * step_count
    rows = step_count * row_count

    everyone = lax.all_gather(attention, "dp", axis=0)
    small = jnp.concatenate(
        [lacking_adapter_lists[:, 0].reshape(step_count, -1), request_slot_index], axis=1
    )
    group = jnp.arange(groups, dtype=jnp.int32)[:, None, None]
    gathered = jnp.where(group == me, small[None], 0)
    for shift in range(1, groups):
        ring = [(i, (i + shift) % groups) for i in range(groups)]
        passed = lax.ppermute(small, "dp", ring)
        gathered = jnp.where(group == (me + groups - shift) % groups, passed[None], gathered)
    small = gathered
    wanted = small[:, :, : owners * per_owner].reshape(batches, owners, per_owner)
    wanted = lax.dynamic_index_in_dim(wanted, me, axis=1, keepdims=False)
    slots = small[:, :, owners * per_owner :] - me * per_owner
    slots = slots.reshape(batches, row_count, 1)

    ends = rows * 3 // 8 // 16 * 16, rows * 25 // 48 // 16 * 16
    flat = attention.reshape(rows, feature_count)
    first = project(flat, output_weight, n, 0, ends[0], 1)
    everyone, first = lax.optimization_barrier((everyone, first))
    shrink = with_adapters(
        shrink_kernel, wanted, everyone.reshape(batches, row_count, feature_count), slots,
        adapter_down_maps, (batches, rank, row_count),
    )

    shrink, flat = lax.optimization_barrier((shrink, flat))
    second = project(flat, output_weight, n, ends[0], ends[1] - ends[0], 2)
    total = lax.psum(shrink, "tensor")
    total, second = lax.optimization_barrier((total, second))
    lora = with_adapters(
        expand_kernel, wanted, total, slots, adapter_up_maps, (batches, row_count, width)
    )

    lora, flat = lax.optimization_barrier((lora, flat))
    third = project(flat, output_weight, n, ends[1], rows - ends[1], 3)
    lora_own = lax.psum_scatter(
        lora.reshape(groups, rows, width), "dp", scatter_dimension=0, tiled=False
    )
    mixed = mix(residual.reshape(rows, width), lora_own, first, second, third)
    return mixed.reshape(residual.shape)


def solution(mesh):
    placed = (
        P(None, ("rep", "dp"), "tensor"),
        P(None, ("rep", "dp"), "tensor"),
        P("tensor", None),
        P("dp", None, "tensor"),
        P("dp", None, "tensor"),
        P(None, ("rep", "dp"), None, None),
        P(None, ("rep", "dp")),
    )
    return jax.shard_map(
        functools.partial(shards, mesh.shape["dp"], mesh.shape["tensor"]),
        mesh=mesh,
        in_specs=placed,
        out_specs=P(None, ("rep", "dp"), "tensor"),
        check_vma=False,
    )
```
